32 devices in a mesh: groups: 2 (over y), row: 4 (over z), col: 4 (over x, core).
Axes of the slice: x: 2, y: 2, z: 4, core: 2. Of those that a mesh axis runs over, the one named last changes fastest.
Arguments:
- three_index: bfloat16 [10, 4096, 1024], P('groups', ('row', 'col')), parts along dimension 0, may hold values from -1.1953125 to 1.1953125
- vir_energy: bfloat16 [8192], P(('groups', 'row', 'col')), parts along dimension 0, may hold values from 0.19921875 to 3
- occ_shell: int32 [10], P('groups'), parts along dimension 0, may hold values from 0 to 7
- shell_energy: float32 [16], P('groups'), parts along dimension 0, may hold values from -2 to -0.4
Outputs:
- gamma: float32 [10, 4096, 1024], P('groups', ('row', 'col')), parts along dimension 0
The draws below stay inside these ranges and needn't reach their ends.
There are 2 independent parts, one for each index of `groups`. The reference program is written for one: setup_inputs(seed, part) draws one part's arguments, and reference() takes and returns one part's arrays. A program takes and returns all parts, laid end to end along the dimension named above; each array names one. Nothing has to cross between parts.
All inputs are finite; a program needn't handle non-finite values.
Results may differ from the reference program's by a relative error of at most 0.00072.
Values may be sent and summed in bfloat16 or wider, within the bound.
A program may use at most 320 MiB of HBM per device.

```python
import jax
import jax.numpy as jnp
from jax import lax

O = 5
V = 4096
Q = 1024
SHELLS = 8


def place_ends(drawn, stream_key, least, top_value):
    place = [jax.random.randint(jax.random.fold_in(stream_key, axis), (), 0, length) for axis, length in enumerate(drawn.shape)]
    longest = drawn.shape.index(max(drawn.shape))
    beside = place[:longest] + [(place[longest] + 1) % drawn.shape[longest]] + place[longest + 1:]
    return drawn.at[tuple(place)].set(least).at[tuple(beside)].set(top_value)


def shard_levels(own_key, extent, shards, least, high):
    def one(dim, shards_of):
        draws = jax.random.uniform(jax.random.fold_in(jax.random.fold_in(own_key, 6), dim), (shards_of,), jnp.float32, least / len(shards), high / len(shards))
        return jnp.repeat(jnp.exp(draws), extent[dim] // shards_of).reshape((-1,) + (1,) * (len(extent) - dim - 1))

    loudness = one(*shards[0])
    for cut in shards[1:]:
        loudness = loudness * one(*cut)
    return loudness


def gaussian(stream_key, dims, scale, limit, split=(), held_as=jnp.bfloat16):
    entries = jax.random.normal(stream_key, dims, jnp.float32) * scale
    if len(split) > 0:
        entries = shard_levels(stream_key, dims, split, -0.22, 0.18) * entries
    return jnp.clip(entries, min=-limit, max=limit).astype(held_as)


def setup_inputs(seed: int = 0, part: int = 0) -> dict:
    seeds = jax.random.split(jax.random.key(seed), 5)
    own_keys = jax.random.split(jax.random.fold_in(seeds[4], part), 5)
    three_index = gaussian(own_keys[0], (O, V, Q), 0.2, 1.1953125, ((1, 16),))
    vir_energy = jnp.clip(0.19921875 + 2.8007812 * jax.random.uniform(own_keys[1], (V,), jnp.float32) ** shard_levels(own_keys[1], (V,), ((0, 16),), -0.2, 0.2), 0.19921875, 3.0).astype(jnp.bfloat16)
    occ_shell = place_ends(jax.random.randint(own_keys[2], (O,), 0, SHELLS), jax.random.fold_in(own_keys[2], 1), 0, SHELLS - 1).astype(jnp.int32)
    shell_energy = jnp.clip(jax.random.uniform(own_keys[3], (SHELLS,), jnp.float32, -2.0, -0.4), -2.0, -0.4)
    return dict(three_index=three_index, vir_energy=vir_energy, occ_shell=occ_shell, shell_energy=shell_energy)


def reference(three_index, vir_energy, occ_shell, shell_energy):
    levels = jnp.arange(SHELLS, dtype=jnp.int32)
    onehot = occ_shell[:, None] == levels[None, :]
    occ_energy = jnp.sum(jnp.where(onehot, shell_energy[None, :], jnp.float32(0.0)), axis=1)
    energies = vir_energy.astype(jnp.float32)
    whole = three_index.astype(jnp.float32)
    width = min(256, V)
    pair_sum = occ_energy[:, None] + occ_energy[None, :]

    def block_gamma(start):
        rows = lax.dynamic_slice_in_dim(whole, start, width, 1)
        row_energy = lax.dynamic_slice_in_dim(energies, start, width, 0)
        coulomb = jnp.einsum('iaq,jbq->ijab', rows, whole)
        denom = pair_sum[:, :, None, None] - row_energy[None, None, :, None] - energies[None, None, None, :]
        amplitude = ((2.0 * coulomb - jnp.swapaxes(coulomb, 0, 1)) / denom).astype(jnp.bfloat16)
        amplitude = lax.optimization_barrier(amplitude).astype(jnp.float32)
        return jnp.einsum('ijab,jbq->iaq', amplitude, whole)

    starts = (jnp.arange(V // width, dtype=jnp.int32) * width).astype(jnp.int32)
    pieces = lax.map(block_gamma, starts)
    return jnp.moveaxis(pieces, 0, 1).reshape(O, V, Q)
```

```python
import functools

import jax
import jax.numpy as jnp
from jax import lax
from jax.experimental import pallas as pl
from jax.experimental.pallas import tpu as pltpu
from jax.sharding import PartitionSpec as P

MESH = pl.DeviceIdType.MESH
PAD = 16
UP, DOWN, ACROSS, TWIN = 0, 1, 2, 3


def occupied_energies(occ_shell, shell_energy):
    levels = jnp.arange(shell_energy.shape[0], dtype=jnp.int32)
    onehot = occ_shell[:, None] == levels[None, :]
    return jnp.sum(jnp.where(onehot, shell_energy[None, :], jnp.float32(0.0)), axis=1)


def gather_and_contract(
    rows, occ, half, occ_ref, b_ref, vir_row_ref, vir_col_ref, out_ref,
    held, coulomb, amp, send_sem, recv_sem,
):
    r = lax.axis_index("row")
    c = lax.axis_index("col")
    k = lax.rem(c, 2)
    x = c // 2
    twin_c = 2 * x + (1 - k)
    across_c = 2 * (1 - x) + k
    size = occ * half
    slots = 2 * (rows - 1) + 1
    has_up, has_down = r + 1 < rows, r > 0

    def chunk_id(row, col, h):
        return (row * 4 + col) * 2 + h

    def copy(row, other_x, h, way):
        col = 2 * jnp.where(other_x == 1, 1 - x, x) + k
        cid = chunk_id(row, col, h)
        device = {UP: {"row": r + 1}, DOWN: {"row": r - 1}, ACROSS: {"col": across_c}, TWIN: {"col": twin_c}}[way]
        return pltpu.make_async_remote_copy(
            src_ref=held.at[cid],
            dst_ref=held.at[cid],
            send_sem=send_sem.at[((row * 2 + other_x) * 2 + h) * 4 + way],
            recv_sem=recv_sem.at[cid],
            device_id=device,
            device_id_type=MESH,
        )

    def arrived(cid):
        pltpu.make_async_remote_copy(
            src_ref=held.at[cid],
            dst_ref=held.at[cid],
            send_sem=send_sem.at[0],
            recv_sem=recv_sem.at[cid],
            device_id={"col": across_c},
            device_id_type=MESH,
        ).wait_recv()

    def event(s, j):
        sign = 2 * lax.rem(j, 2) - 1
        over_col = j // 2
        last = s == slots - 1
        late = jnp.maximum(s - 1, 0)
        d_row = jnp.where(last, 1, 1 + s // 2)
        h_row = jnp.where(last, 1, lax.rem(s, 2))
        d_col = jnp.where(s < 2, 0, 1 + late // 2)
        h_col = jnp.where(s < 2, s, lax.rem(late, 2))
        d_col = jnp.where(s == 2, 1, d_col)
        h_col = jnp.where(s == 2, 0, h_col)
        d = jnp.where(over_col == 1, d_col, d_row)
        h = jnp.where(over_col == 1, h_col, h_row)
        other_x = jnp.where((over_col == 1) | last, 1, 0)
        row = r + sign * d
        valid = (row >= 0) & (row < rows) & ((d > 0) | (sign > 0))
        return row, other_x, d, h, sign, valid

    def own(act):
        for h in range(2):
            pl.when(has_up)(lambda h=h: act(copy(r, 0, h, UP)))
            pl.when(has_down)(lambda h=h: act(copy(r, 0, h, DOWN)))
            act(copy(r, 0, h, ACROSS))
            act(copy(r, 0, h, TWIN))

    def onward(row, other_x, d, h, sign, valid, act):
        line = valid & (other_x == 0)
        pl.when(line & (sign < 0) & has_up)(lambda: act(copy(row, 0, h, UP)))
        pl.when(line & (sign > 0) & has_down)(lambda: act(copy(row, 0, h, DOWN)))
        pl.when(line & ((d > 1) | (h == 0)))(lambda: act(copy(row, 0, h, ACROSS)))
        pl.when(valid)(lambda: act(copy(row, other_x, h, TWIN)))

    def extra(act):
        pl.when(has_up)(lambda: act(copy(r, 1, 1, UP)))
        pl.when(has_down)(lambda: act(copy(r, 1, 1, DOWN)))

    start = lambda desc: desc.start()
    sent = lambda desc: desc.wait_send()

    mine = chunk_id(r, c, 0)
    for h in range(2):
        for i in range(occ):
            held[mine + h, i * half:(i + 1) * half, :] = b_ref[i, h * half:(h + 1) * half, :]
        held[mine + h, size:size + PAD, :] = jnp.zeros((PAD, held.shape[-1]), held.dtype)
        held[mine + h, size:size + PAD, :half] = jnp.broadcast_to(vir_row_ref[h:h + 1, :], (PAD, half))

    barrier = pltpu.get_barrier_semaphore()

    def greet(device):
        pl.semaphore_signal(barrier, inc=1, device_id=device, device_id_type=MESH)

    pl.when(has_up)(lambda: greet({"row": r + 1}))
    pl.when(has_down)(lambda: greet({"row": r - 1}))
    greet({"col": across_c})
    greet({"col": twin_c})
    pl.semaphore_wait(barrier, 2 + has_up.astype(jnp.int32) + has_down.astype(jnp.int32))

    own(start)
    out_ref[...] = jnp.zeros_like(out_ref)

    def contract(cid):
        vir_b = held[cid, size:size + PAD, :half][:1].astype(jnp.float32)
        for t in range(2):
            coulomb[t] = lax.dot_general(
                held[mine + t, :size, :], held[cid, :size, :],
                (((1,), (1,)), ((), ())), preferred_element_type=jnp.float32,
            )
        for t in range(2):
            vir_a = vir_col_ref[t * half:(t + 1) * half, :]
            for i in range(occ):
                for j in range(i + 1):
                    inverse = 1.0 / (((occ_ref[i] + occ_ref[j]) - vir_a) - vir_b)
                    ij = coulomb[t, i * half:(i + 1) * half, j * half:(j + 1) * half]
                    if i == j:
                        amp[t, i * half:(i + 1) * half, j * half:(j + 1) * half] = ((2.0 * ij - ij) * inverse).astype(jnp.bfloat16)
                        continue
                    ji = coulomb[t, j * half:(j + 1) * half, i * half:(i + 1) * half]
                    amp[t, i * half:(i + 1) * half, j * half:(j + 1) * half] = ((2.0 * ij - ji) * inverse).astype(jnp.bfloat16)
                    amp[t, j * half:(j + 1) * half, i * half:(i + 1) * half] = ((2.0 * ji - ij) * inverse).astype(jnp.bfloat16)
        for t in range(2):
            out_ref[t] += jnp.dot(amp[t], held[cid, :size, :], preferred_element_type=jnp.float32)

    @pl.loop(0, slots + 1)
    def _(step):
        s = step - 1
        later = jnp.maximum(s, 0)

        @pl.when(step > 0)
        def _():
            @pl.loop(0, 4)
            def _(j):
                row, other_x, d, h, sign, valid = event(later, j)
                col = 2 * jnp.where(other_x == 1, 1 - x, x) + k

                @pl.when(valid)
                def _():
                    arrived(chunk_id(row, col, h))

                onward(row, other_x, d, h, sign, valid, start)

            pl.when(s == 3)(lambda: extra(start))

        @pl.loop(0, 8)
        def _(u):
            row, other_x, _, h, _, valid = event(later, lax.rem(u, 4))
            first = step == 0
            core = jnp.where(u // 4 == 0, k, 1 - k)
            row = jnp.where(first, r, row)
            other_x = jnp.where(first, 0, other_x)
            h = jnp.where(first, lax.rem(u, 2), h)
            go = jnp.where(first, (lax.rem(u, 4) < 2).astype(jnp.int32), valid.astype(jnp.int32)) == 1
            cid = chunk_id(row, 2 * jnp.where(other_x == 1, 1 - x, x) + core, h)

            @pl.when(go)
            def _():
                pl.when(u >= 4)(lambda: arrived(cid))
                contract(cid)

    own(sent)
    extra(sent)

    @pl.loop(0, slots)
    def _(s):
        @pl.loop(0, 4)
        def _(j):
            onward(*event(s, j), sent)


def chip_plan(rows, three_index, vir_energy, occ_shell, shell_energy):
    occ, virtuals, aux = three_index.shape
    half = virtuals // 2
    size = occ * half
    chunks = rows * 4 * 2
    vmem = pl.BlockSpec(memory_space=pltpu.VMEM)
    gamma = pl.pallas_call(
        functools.partial(gather_and_contract, rows, occ, half),
        out_shape=jax.ShapeDtypeStruct((2, size, aux), jnp.float32),
        in_specs=[pl.BlockSpec(memory_space=pltpu.SMEM), vmem, vmem, vmem],
        out_specs=vmem,
        scratch_shapes=[
            pltpu.VMEM((chunks, size + PAD, aux), jnp.bfloat16),
            pltpu.VMEM((2, size, size), jnp.float32),
            pltpu.VMEM((2, size, size), jnp.bfloat16),
            pltpu.SemaphoreType.DMA((rows * 2 * 2 * 4,)),
            pltpu.SemaphoreType.DMA((chunks,)),
        ],
        compiler_params=pltpu.CompilerParams(
            collective_id=0, has_side_effects=True, vmem_limit_bytes=62 * 1024 * 1024
        ),
    )(
        occupied_energies(occ_shell, shell_energy),
        three_index,
        vir_energy.reshape(2, half),
        vir_energy.astype(jnp.float32).reshape(virtuals, 1),
    )
    gamma = gamma.reshape(2, occ, half, aux)
    return jnp.swapaxes(gamma, 0, 1).reshape(occ, virtuals, aux)


def gathered_plan(three_index, vir_energy, occ_shell, shell_energy):
    occ_energy = occupied_energies(occ_shell, shell_energy)
    pair_sum = occ_energy[:, None] + occ_energy[None, :]
    energy_row = vir_energy[None, :]
    own_block, own_energy = (
        lax.all_gather(three_index, "col", axis=1, tiled=True),
        lax.all_gather(energy_row, "col", axis=1, tiled=True),
    )
    own_energy = own_energy[0].astype(jnp.float32)
    partner_all, energy_all = (
        lax.all_gather(three_index, "row", axis=1, tiled=True),
        lax.all_gather(energy_row, "row", axis=1, tiled=True),
    )
    coulomb = jnp.einsum(
        "iaq,jbq->ijab", own_block, partner_all, preferred_element_type=jnp.float32
    )
    denom = (
        pair_sum[:, :, None, None]
        - own_energy[None, None, :, None]
        - energy_all[0].astype(jnp.float32)[None, None, None, :]
    )
    amplitude = ((2.0 * coulomb - jnp.swapaxes(coulomb, 0, 1)) / denom).astype(jnp.bfloat16)
    partial_sum = jnp.einsum(
        "ijab,jbq->iaq", amplitude, partner_all, preferred_element_type=jnp.float32
    )
    return lax.psum_scatter(partial_sum, "col", scatter_dimension=1, tiled=True)


def solution(mesh):
    rows, cols = mesh.shape["row"], mesh.shape["col"]
    fits = rows == 4 and cols == 4
    plan = functools.partial(chip_plan, rows) if fits else gathered_plan
    in_specs = (
        P("groups", ("row", "col"), None),
        P(("groups", "row", "col")),
        P("groups"),
        P("groups"),
    )
    out_specs = P("groups", ("row", "col"), None)
    return jax.shard_map(
        plan, mesh=mesh, in_specs=in_specs, out_specs=out_specs, check_vma=False
    )
```

```python
import functools

import jax
import jax.numpy as jnp
from jax import lax
from jax.experimental import pallas as pl
from jax.experimental.pallas import tpu as pltpu
from jax.sharding import PartitionSpec as P

MESH = pl.DeviceIdType.MESH
PAD = 16
UP, DOWN, ACROSS, TWIN = 0, 1, 2, 3


def occupied_energies(occ_shell, shell_energy):
    levels = jnp.arange(shell_energy.shape[0], dtype=jnp.int32)
    onehot = occ_shell[:, None] == levels[None, :]
    return jnp.sum(jnp.where(onehot, shell_energy[None, :], jnp.float32(0.0)), axis=1)


def gather_and_contract(
    rows, occ, half, occ_ref, b_ref, vir_row_ref, vir_col_ref, out_ref,
    held, held_vir, coulomb, amp, send_sem, recv_sem, send_vir_sem, recv_vir_sem,
):
    r = lax.axis_index("row")
    c = lax.axis_index("col")
    k = lax.rem(c, 2)
    x = c // 2
    twin_c = 2 * x + (1 - k)
    across_c = 2 * (1 - x) + k
    size = occ * half
    slots = 2 * (rows - 1) + 1
    has_up, has_down = r + 1 < rows, r > 0

    def chunk_id(row, col, h):
        return (row * 4 + col) * 2 + h

    def copy(row, other_x, h, way):
        col = 2 * jnp.where(other_x == 1, 1 - x, x) + k
        cid = chunk_id(row, col, h)
        device = {UP: {"row": r + 1}, DOWN: {"row": r - 1}, ACROSS: {"col": across_c}, TWIN: {"col": twin_c}}[way]
        return chunk_copies(cid, ((row * 2 + other_x) * 2 + h) * 4 + way, device)

    def chunk_copies(cid, out, device):
        return [
            pltpu.make_async_remote_copy(
                src_ref=ref.at[cid],
                dst_ref=ref.at[cid],
                send_sem=sends.at[out],
                recv_sem=receives.at[cid],
                device_id=device,
                device_id_type=MESH,
            )
            for ref, sends, receives in (
                (held_vir, send_vir_sem, recv_vir_sem),
                (held, send_sem, recv_sem),
            )
        ]

    def arrived(cid):
        for desc in chunk_copies(cid, 0, {"col": across_c}):
            desc.wait_recv()

    def event(s, j):
        sign = 2 * lax.rem(j, 2) - 1
        over_col = j // 2
        last = s == slots - 1
        late = jnp.maximum(s - 1, 0)
        d_row = jnp.where(last, 1, 1 + s // 2)
        h_row = jnp.where(last, 1, lax.rem(s, 2))
        d_col = jnp.where(s < 2, 0, 1 + late // 2)
        h_col = jnp.where(s < 2, s, lax.rem(late, 2))
        d_col = jnp.where(s == 2, 1, d_col)
        h_col = jnp.where(s == 2, 0, h_col)
        d = jnp.where(over_col == 1, d_col, d_row)
        h = jnp.where(over_col == 1, h_col, h_row)
        other_x = jnp.where((over_col == 1) | last, 1, 0)
        row = r + sign * d
        valid = (row >= 0) & (row < rows) & ((d > 0) | (sign > 0))
        return row, other_x, d, h, sign, valid

    def own(act):
        for h in range(2):
            pl.when(has_up)(lambda h=h: act(copy(r, 0, h, UP)))
            pl.when(has_down)(lambda h=h: act(copy(r, 0, h, DOWN)))
            act(copy(r, 0, h, ACROSS))
            act(copy(r, 0, h, TWIN))

    def onward(row, other_x, d, h, sign, valid, act):
        line = valid & (other_x == 0)
        pl.when(line & (sign < 0) & has_up)(lambda: act(copy(row, 0, h, UP)))
        pl.when(line & (sign > 0) & has_down)(lambda: act(copy(row, 0, h, DOWN)))
        pl.when(line & ((d > 1) | (h == 0)))(lambda: act(copy(row, 0, h, ACROSS)))
        pl.when(valid)(lambda: act(copy(row, other_x, h, TWIN)))

    def extra(act):
        pl.when(has_up)(lambda: act(copy(r, 1, 1, UP)))
        pl.when(has_down)(lambda: act(copy(r, 1, 1, DOWN)))

    def start(pair):
        for desc in pair:
            desc.start()

    def sent(pair):
        for desc in pair:
            desc.wait_send()


    mine = chunk_id(r, c, 0)
    for h in range(2):
        for i in range(occ):
            held[mine + h, i * half:(i + 1) * half, :] = b_ref[i, h * half:(h + 1) * half, :]
        held_vir[mine + h] = jnp.broadcast_to(vir_row_ref[h:h + 1, :], (PAD, half))

    barrier = pltpu.get_barrier_semaphore()

    def greet(device):
        pl.semaphore_signal(barrier, inc=1, device_id=device, device_id_type=MESH)

    pl.when(has_up)(lambda: greet({"row": r + 1}))
    pl.when(has_down)(lambda: greet({"row": r - 1}))
    greet({"col": across_c})
    greet({"col": twin_c})
    pl.semaphore_wait(barrier, 2 + has_up.astype(jnp.int32) + has_down.astype(jnp.int32))

    own(start)
    out_ref[...] = jnp.zeros_like(out_ref)

    def contract(cid):
        vir_b = held_vir[cid][:1].astype(jnp.float32)
        for t in range(2):
            coulomb[t] = lax.dot_general(
                held[mine + t], held[cid],
                (((1,), (1,)), ((), ())), preferred_element_type=jnp.float32,
            )
        for t in range(2):
            vir_a = vir_col_ref[t * half:(t + 1) * half, :]
            for i in range(occ):
                for j in range(i + 1):
                    inverse = 1.0 / (((occ_ref[i] + occ_ref[j]) - vir_a) - vir_b)
                    ij = coulomb[t, i * half:(i + 1) * half, j * half:(j + 1) * half]
                    if i == j:
                        amp[t, i * half:(i + 1) * half, j * half:(j + 1) * half] = ((2.0 * ij - ij) * inverse).astype(jnp.bfloat16)
                        continue
                    ji = coulomb[t, j * half:(j + 1) * half, i * half:(i + 1) * half]
                    amp[t, i * half:(i + 1) * half, j * half:(j + 1) * half] = ((2.0 * ij - ji) * inverse).astype(jnp.bfloat16)
                    amp[t, j * half:(j + 1) * half, i * half:(i + 1) * half] = ((2.0 * ji - ij) * inverse).astype(jnp.bfloat16)
        for t in range(2):
            out_ref[t] += jnp.dot(amp[t], held[cid], preferred_element_type=jnp.float32)

    def receive(s, j):
        row, other_x, d, h, sign, valid = event(s, j)
        col = 2 * jnp.where(other_x == 1, 1 - x, x) + k

        @pl.when(valid)
        def _():
            arrived(chunk_id(row, col, h))

        onward(row, other_x, d, h, sign, valid, start)

    @pl.loop(0, slots + 1)
    def _(step):
        s = step - 1
        later = jnp.maximum(s, 0)

        @pl.when((step > 0) & (s < slots - 1))
        def _():
            @pl.loop(0, 4)
            def _(j):
                receive(later, j)

            pl.when(s == 3)(lambda: extra(start))

        @pl.loop(0, 8)
        def _(u):
            first = step == 0
            last = s == slots - 1
            j = jnp.where(last, lax.rem(u, 2) + 2 * (u // 4), lax.rem(u, 4))
            twin = jnp.where(last, lax.rem(u // 2, 2), u // 4)
            pl.when(last & (twin == 0))(lambda: receive(later, j))
            row, other_x, _, h, _, valid = event(later, j)
            core = jnp.where(twin == 0, k, 1 - k)
            row = jnp.where(first, r, row)
            other_x = jnp.where(first, 0, other_x)
            h = jnp.where(first, lax.rem(u, 2), h)
            go = jnp.where(first, (lax.rem(u, 4) < 2).astype(jnp.int32), valid.astype(jnp.int32)) == 1
            cid = chunk_id(row, 2 * jnp.where(other_x == 1, 1 - x, x) + core, h)

            @pl.when(go)
            def _():
                pl.when(twin == 1)(lambda: arrived(cid))
                contract(cid)

    own(sent)
    extra(sent)

    @pl.loop(0, slots)
    def _(s):
        @pl.loop(0, 4)
        def _(j):
            onward(*event(s, j), sent)


def chip_plan(rows, three_index, vir_energy, occ_shell, shell_energy):
    occ, virtuals, aux = three_index.shape
    half = virtuals // 2
    size = occ * half
    chunks = rows * 4 * 2
    vmem = pl.BlockSpec(memory_space=pltpu.VMEM)
    gamma = pl.pallas_call(
        functools.partial(gather_and_contract, rows, occ, half),
        out_shape=jax.ShapeDtypeStruct((2, size, aux), jnp.float32),
        in_specs=[pl.BlockSpec(memory_space=pltpu.SMEM), vmem, vmem, vmem],
        out_specs=vmem,
        scratch_shapes=[
            pltpu.VMEM((chunks, size, aux), jnp.bfloat16),
            pltpu.VMEM((chunks, PAD, half), jnp.bfloat16),
            pltpu.VMEM((2, size, size), jnp.float32),
            pltpu.VMEM((2, size, size), jnp.bfloat16),
            pltpu.SemaphoreType.DMA((rows * 2 * 2 * 4,)),
            pltpu.SemaphoreType.DMA((chunks,)),
            pltpu.SemaphoreType.DMA((rows * 2 * 2 * 4,)),
            pltpu.SemaphoreType.DMA((chunks,)),
        ],
        compiler_params=pltpu.CompilerParams(
            collective_id=0, has_side_effects=True, vmem_limit_bytes=62 * 1024 * 1024
        ),
    )(
        occupied_energies(occ_shell, shell_energy),
        three_index,
        vir_energy.reshape(2, half),
        vir_energy.astype(jnp.float32).reshape(virtuals, 1),
    )
    gamma = gamma.reshape(2, occ, half, aux)
    return jnp.swapaxes(gamma, 0, 1).reshape(occ, virtuals, aux)


def gathered_plan(three_index, vir_energy, occ_shell, shell_energy):
    occ_energy = occupied_energies(occ_shell, shell_energy)
    pair_sum = occ_energy[:, None] + occ_energy[None, :]
    energy_row = vir_energy[None, :]
    own_block, own_energy = (
        lax.all_gather(three_index, "col", axis=1, tiled=True),
        lax.all_gather(energy_row, "col", axis=1, tiled=True),
    )
    own_energy = own_energy[0].astype(jnp.float32)
    partner_all, energy_all = (
        lax.all_gather(three_index, "row", axis=1, tiled=True),
        lax.all_gather(energy_row, "row", axis=1, tiled=True),
    )
    coulomb = jnp.einsum(
        "iaq,jbq->ijab", own_block, partner_all, preferred_element_type=jnp.float32
    )
    denom = (
        pair_sum[:, :, None, None]
        - own_energy[None, None, :, None]
        - energy_all[0].astype(jnp.float32)[None, None, None, :]
    )
    amplitude = ((2.0 * coulomb - jnp.swapaxes(coulomb, 0, 1)) / denom).astype(jnp.bfloat16)
    partial_sum = jnp.einsum(
        "ijab,jbq->iaq", amplitude, partner_all, preferred_element_type=jnp.float32
    )
    return lax.psum_scatter(partial_sum, "col", scatter_dimension=1, tiled=True)


def solution(mesh):
    rows, cols = mesh.shape["row"], mesh.shape["col"]
    fits = rows == 4 and cols == 4
    plan = functools.partial(chip_plan, rows) if fits else gathered_plan
    in_specs = (
        P("groups", ("row", "col"), None),
        P(("groups", "row", "col")),
        P("groups"),
        P("groups"),
    )
    out_specs = P("groups", ("row", "col"), None)
    return jax.shard_map(
        plan, mesh=mesh, in_specs=in_specs, out_specs=out_specs, check_vma=False
    )
```
